32 devices in a mesh: pair: 16 (over z, x, core), grp: 2 (over y).
Axes of the slice: x: 2, y: 2, z: 4, core: 2. Of those that a mesh axis runs over, the one named last changes fastest.
Arguments:
- amplitudes: float32 [2, 112, 2048], P('grp', 'pair'), may hold values from -6 to 6
- integrals: float32 [2048, 32768], P('grp', 'pair'), may hold values from -0.375 to 0.375
- owner_blocks: int32 [16], replicated, may hold values from 0 to 15, each once
- occ_pairs: int32 [2, 2, 112], P('grp'), may hold values from 0 to 63, as said below
- vir_pairs: int32 [2, 32768], replicated, may hold values from 0 to 511, as said below
- occ_energy: float32 [64], replicated, may hold values from -1.5 to -0.5
- vir_energy: float32 [512], replicated, may hold values from 0.2 to 1.5
Outputs:
- ladder: float32 [2, 112, 32768], P('grp', 'pair')
The draws below stay inside these ranges and needn't reach their ends.
Inputs may be any that keep to these rules, and one draw needn't show every extreme that they name: `occ_pairs`: each column is a pair i<j; no pair occurs twice. `vir_pairs`: each column is a pair a<b; no pair occurs twice. `owner_blocks`: a permutation.
All inputs are finite; a program needn't handle non-finite values.
Results may differ from the reference program's by a relative error of at most 0.000071.
Values sent between devices are 32-bit elements; how exact they have to be, the bound alone decides.
A program may use at most 64 MiB of HBM per device.

```python
import jax
import jax.numpy as jnp
import numpy as np
from jax import lax

NOCC = 64
NVIR = 512
CD = 2048
BLOCKS = 16
IJ_G = 112
IJ = 224
AB = 32768
N_GRP = 2


def draw_occ_pairs(key, part):
    first, second = np.triu_indices(NOCC, 1)
    table = jnp.asarray(np.stack([first, second]), dtype=jnp.int32)
    picked = jax.random.permutation(key, table.shape[1])[:IJ]
    chosen = jnp.take(table, picked, axis=1)
    return jnp.transpose(chosen.reshape(2, -1, IJ_G), (1, 0, 2)).astype(jnp.int32)


def draw_vir_pairs(key, part):
    first, second = np.triu_indices(NVIR, 1)
    table = jnp.asarray(np.stack([first, second]), dtype=jnp.int32)
    picked = jax.random.permutation(jax.random.fold_in(key, 7), table.shape[1])[:AB]
    return jnp.take(table, picked, axis=1).astype(jnp.int32)


def block_levels(rng, extent, shards, smallest, top_value):
    gain = 1.0
    for dim, parts in shards:
        steps = jax.random.uniform(jax.random.fold_in(jax.random.fold_in(rng, 6), dim), (parts,), jnp.float32, smallest / len(shards), top_value / len(shards))
        gain = gain * jnp.repeat(jnp.exp(steps), extent[dim] // parts).reshape((-1,) + (1,) * (len(extent) - 1 - dim))
    return gain


def centred(own_key, extent, scale, most, cuts=(), kind=jnp.bfloat16):
    level = block_levels(own_key, extent, cuts, -0.22, 0.18) if cuts else 1.0
    result = jax.random.normal(own_key, extent, jnp.float32) * scale * level
    return jnp.minimum(jnp.maximum(result, -most), most).astype(kind)


def setup_inputs(seed: int = 0) -> dict:
    streams_of = jax.random.split(jax.random.key(seed), 8)
    return {
        "amplitudes": centred(streams_of[0], (N_GRP, IJ_G, CD), 1.0, 6.0, ((0, 2), (1, 16)), jnp.float32),
        "integrals": centred(streams_of[1], (CD, AB), (CD // 8) ** -0.5, 0.375, ((0, 2), (1, 16)), jnp.float32),
        "owner_blocks": jax.random.permutation(streams_of[2], BLOCKS).astype(jnp.int32),
        "occ_pairs": draw_occ_pairs(jax.random.fold_in(streams_of[7], 71), 0),
        "vir_pairs": draw_vir_pairs(jax.random.fold_in(streams_of[7], 71), 0),
        "occ_energy": jnp.clip(jax.random.uniform(streams_of[5], (NOCC,), jnp.float32, -1.5, -0.5), -1.5, -0.5),
        "vir_energy": jnp.clip(jax.random.uniform(streams_of[6], (NVIR,), jnp.float32, 0.2, 1.5), 0.2, 1.5),
    }


def reference(amplitudes, integrals, owner_blocks, occ_pairs, vir_pairs, occ_energy, vir_energy):
    groups = amplitudes.shape[0]
    width = amplitudes.shape[2]
    nblocks = owner_blocks.shape[0]
    tau = amplitudes.reshape(-1, nblocks, width // nblocks)
    permuted = jnp.take(tau, owner_blocks, axis=1).reshape(-1, width)
    work = jnp.dot(permuted, integrals, precision=lax.Precision.HIGHEST, preferred_element_type=jnp.float32)
    occ_flat = jnp.transpose(occ_pairs, (1, 0, 2)).reshape(2, -1)
    occ_sum = jnp.take(occ_energy, occ_flat[0]) + jnp.take(occ_energy, occ_flat[1])
    vir_sum = jnp.take(vir_energy, vir_pairs[0]) + jnp.take(vir_energy, vir_pairs[1])
    ladder = work / (occ_sum[:, None] - vir_sum[None, :])
    return ladder.reshape(groups, amplitudes.shape[1], -1)
```

```python
import functools

import jax
import jax.numpy as jnp
from jax import lax
from jax.experimental import pallas as pl
from jax.experimental.pallas import tpu as pltpu
from jax.sharding import PartitionSpec as P

LANES = 128
PAD = 8
MESH = pl.DeviceIdType.MESH


def pair_energies(energy, pairs):
    return jnp.take(energy, pairs[0]) + jnp.take(energy, pairs[1])


def flip(bit, on):
    return 1 - bit if on else bit


def split_bf16(x):
    hi = x.astype(jnp.bfloat16)
    return hi, (x - hi.astype(jnp.float32)).astype(jnp.bfloat16)


def kernel(
    owner_ref, occ_pairs_ref, occ_energy_ref, amp_ref, vir_energy_ref, vir_pairs_ref, integrals_ref,
    out_ref,
    gath, other, raw, rhs_hi, rhs_lo, vp, virs, lhs_f, lhs_hi, lhs_lo, ysend, yrecv, own, piece,
    load_sem, vp_sem, yamp_sem, asend_sem, arecv_sem, ysend_sem, yrecv_sem, osend_sem, orecv_sem, self_sem,
):
    npair = out_ref.shape[1] // own.shape[2]
    rows = out_ref.shape[0]
    depth, cols = integrals_ref.shape
    kb = depth // LANES
    nb = cols // LANES
    nv = vir_energy_ref.shape[1]
    me = lax.axis_index("pair")
    g = lax.axis_index("grp")
    og = 1 - g
    core = me % 2
    x = (me // 2) % 2
    z = me // 4
    zb0, zb1 = z % 2, z // 2

    def at(k):
        return flip(zb1, k & 8) * 8 + flip(zb0, k & 4) * 4 + flip(x, k & 2) * 2 + flip(core, k & 1)

    nload = 4
    step = depth // nload
    loads = [
        pltpu.make_async_copy(
            integrals_ref.at[pl.ds(i * step, step)], raw.at[pl.ds(i * step, step)], load_sem.at[i]
        )
        for i in range(nload)
    ]
    vp_copy = pltpu.make_async_copy(vir_pairs_ref.at[:, pl.ds(pl.multiple_of(me * cols, cols), cols)], vp, vp_sem)
    vp_copy.start()
    for c in loads:
        c.start()

    barrier = pltpu.get_barrier_semaphore()
    pl.semaphore_signal(barrier, inc=1, device_id=(me, og), device_id_type=MESH)
    for k in range(1, npair):
        pl.semaphore_signal(barrier, inc=1, device_id=(at(k), g), device_id_type=MESH)

    for b in range(kb):
        other[:, b, :] = amp_ref[:, owner_ref[og * kb + b], :]
        gath[me, g, :, b, :] = amp_ref[:, owner_ref[g * kb + b], :]
    lhs_f[...] = jnp.zeros_like(lhs_f)

    pl.semaphore_wait(barrier, npair)

    yamp = pltpu.make_async_remote_copy(
        src_ref=other, dst_ref=gath.at[me, g], send_sem=yamp_sem.at[0], recv_sem=yamp_sem.at[1],
        device_id=(me, og), device_id_type=MESH,
    )
    yamp.start()

    vp_copy.wait()
    e = vir_energy_ref[...]
    e0 = e.astype(jnp.bfloat16).astype(jnp.float32)
    e1 = (e - e0).astype(jnp.bfloat16).astype(jnp.float32)
    e2 = e - e0 - e1
    rid = lax.broadcasted_iota(jnp.int32, (16, nv), 0)
    e3 = jnp.where(rid == 0, e0, jnp.where(rid == 1, e1, jnp.where(rid == 2, e2, 0.0))).astype(jnp.bfloat16)
    tv = 512
    for t in range(cols // tv):
        a = vp[0:1, t * tv:(t + 1) * tv]
        b = vp[1:2, t * tv:(t + 1) * tv]
        ids = lax.broadcasted_iota(jnp.int32, (nv, tv), 0)
        hot = jnp.where((ids == a) | (ids == b), 1.0, 0.0).astype(jnp.bfloat16)
        v = jnp.sum(jnp.dot(e3, hot, preferred_element_type=jnp.float32), axis=0, keepdims=True)
        for j in range(tv // LANES):
            q = t * (tv // LANES) + j
            virs[q:q + 1, :] = v[:, j * LANES:(j + 1) * LANES]

    yamp.wait()

    def amp_copy(block, target, slot):
        return pltpu.make_async_remote_copy(
            src_ref=gath.at[block], dst_ref=gath.at[block], send_sem=asend_sem.at[slot], recv_sem=arecv_sem.at[block],
            device_id=(target, g), device_id_type=MESH,
        )

    def split_rhs(i):
        loads[i].wait()
        h = step // 2
        for s in (i * step, i * step + h):
            hi, lo = split_bf16(raw[s:s + h, :])
            rhs_hi[s:s + h, :] = hi
            rhs_lo[s:s + h, :] = lo

    sends = []

    def send(rel, hop):
        c = amp_copy(at(rel), at(hop), len(sends))
        c.start()
        sends.append(c)

    def arrived(rel):
        amp_copy(at(rel), at(rel), 0).wait_recv()

    for k in (12, 8, 4, 2, 1):
        send(0, k)
    split_rhs(0)
    split_rhs(1)
    for i, k in enumerate((4, 8, 12)):
        arrived(k)
        send(k, 2)
        send(k, 1)
        if i == 0:
            split_rhs(2)
    split_rhs(3)
    for k in (2, 6, 10, 14):
        arrived(k)
        send(k, 1)
    for k in (1, 5, 9, 13, 3, 7, 11, 15):
        arrived(k)

    for p in range(npair):
        for b in range(kb):
            for h in range(2):
                lhs_f[h * npair * PAD + p * PAD:h * npair * PAD + p * PAD + rows, b * LANES:(b + 1) * LANES] = (
                    gath[p, h, :, b, :]
                )
    hi, lo = split_bf16(lhs_f[...])
    lhs_hi[...] = hi
    lhs_lo[...] = lo

    half = npair * PAD
    tn = 512

    def multiply(group, target):
        left_hi = lhs_hi[pl.ds(pl.multiple_of(group * half, half), half), :]
        left_lo = lhs_lo[pl.ds(pl.multiple_of(group * half, half), half), :]
        both = jnp.concatenate([left_hi, left_lo], axis=0)
        for t in range(cols // tn):
            right = rhs_hi[:, t * tn:(t + 1) * tn]
            r = jnp.dot(both, right, preferred_element_type=jnp.float32)
            r = r[:half] + r[half:] + jnp.dot(
                left_hi, rhs_lo[:, t * tn:(t + 1) * tn], preferred_element_type=jnp.float32
            )
            for p in range(npair):
                for j in range(tn // LANES):
                    target[p, :, t * (tn // LANES) + j, :] = r[p * PAD:p * PAD + rows, j * LANES:(j + 1) * LANES]

    def part_copy(p):
        return pltpu.make_async_remote_copy(
            src_ref=ysend.at[p], dst_ref=yrecv.at[p], send_sem=ysend_sem.at[p], recv_sem=yrecv_sem.at[p],
            device_id=(me, og), device_id_type=MESH,
        )

    order = (12, 13, 14, 15, 8, 9, 10, 11, 4, 5, 6, 7, 2, 3, 1, 0)
    multiply(og, ysend)
    for k in order:
        part_copy(at(k)).start()
    multiply(g, own)

    def out_copy(p, source):
        return pltpu.make_async_remote_copy(
            src_ref=piece.at[p], dst_ref=out_ref.at[:, pl.ds(pl.multiple_of(source * nb, nb), nb), :],
            send_sem=osend_sem.at[p], recv_sem=orecv_sem.at[source],
            device_id=(p, g), device_id_type=MESH,
        )

    vir = virs[...]
    for k in order:
        p = at(k)
        part_copy(p).wait_recv()
        for r in range(rows):
            row = p * rows + r
            occ = occ_energy_ref[occ_pairs_ref[0, row]] + occ_energy_ref[occ_pairs_ref[1, row]]
            piece[p, r] = (own[p, r] + yrecv[p, r]) / (occ - vir)
        if k:
            out_copy(p, me).start()
    mine = pltpu.make_async_copy(
        piece.at[me], out_ref.at[:, pl.ds(pl.multiple_of(me * nb, nb), nb), :], self_sem
    )
    mine.start()
    for c in sends:
        c.wait_send()
    for k in range(npair):
        part_copy(at(k)).wait_send()
    mine.wait()
    for k in range(1, npair):
        out_copy(at(k), at(k)).wait_recv()
    for k in range(1, npair):
        out_copy(at(k), me).wait_send()


def two_groups(amplitudes, integrals, owner_blocks, occ_pairs, vir_pairs, occ_energy, vir_energy):
    npair = lax.axis_size("pair")
    rows, width = amplitudes.shape[1:]
    depth, cols = integrals.shape
    kb, nb = depth // LANES, cols // LANES
    nv = vir_energy.shape[0]
    if rows > PAD or owner_blocks.shape[0] != 2 * kb or cols % 512:
        return any_groups(amplitudes, integrals, owner_blocks, occ_pairs, vir_pairs, occ_energy, vir_energy)
    f32, bf16 = jnp.float32, jnp.bfloat16
    dma = pltpu.SemaphoreType.DMA
    vmem = pl.BlockSpec(memory_space=pltpu.VMEM)
    smem = pl.BlockSpec(memory_space=pltpu.SMEM)
    hbm = pl.BlockSpec(memory_space=pl.ANY)
    out = pl.pallas_call(
        kernel,
        out_shape=jax.ShapeDtypeStruct((rows, npair * nb, LANES), f32),
        in_specs=[smem, smem, smem, vmem, vmem, hbm, hbm],
        out_specs=hbm,
        scratch_shapes=[
            pltpu.VMEM((npair, 2, rows, kb, LANES), f32),
            pltpu.VMEM((rows, kb, LANES), f32),
            pltpu.VMEM((depth, cols), f32),
            pltpu.VMEM((depth, cols), bf16),
            pltpu.VMEM((depth, cols), bf16),
            pltpu.VMEM((2, cols), jnp.int32),
            pltpu.VMEM((nb, LANES), f32),
            pltpu.VMEM((2 * npair * PAD, depth), f32),
            pltpu.VMEM((2 * npair * PAD, depth), bf16),
            pltpu.VMEM((2 * npair * PAD, depth), bf16),
            pltpu.VMEM((npair, rows, nb, LANES), f32),
            pltpu.VMEM((npair, rows, nb, LANES), f32),
            pltpu.VMEM((npair, rows, nb, LANES), f32),
            pltpu.VMEM((npair, rows, nb, LANES), f32),
            dma((4,)), dma, dma((2,)), dma((16,)), dma((npair,)),
            dma((npair,)), dma((npair,)), dma((npair,)), dma((npair,)), dma,
        ],
        compiler_params=pltpu.CompilerParams(
            collective_id=0, has_side_effects=True, vmem_limit_bytes=48 * 1024 * 1024
        ),
        cost_estimate=pl.CostEstimate(
            flops=12 * npair * rows * depth * cols, bytes_accessed=4 * depth * cols, transcendentals=0
        ),
    )(
        owner_blocks, occ_pairs[0], occ_energy, amplitudes.reshape(rows, width // LANES, LANES),
        vir_energy.reshape(1, nv), vir_pairs, integrals,
    )
    return out.reshape(1, rows, npair * cols)


def any_groups(amplitudes, integrals, owner_blocks, occ_pairs, vir_pairs, occ_energy, vir_energy):
    block = integrals.shape[0]
    columns = integrals.shape[1]
    groups = lax.axis_size("grp")
    nblocks = owner_blocks.shape[0]
    sub_width = block * groups // nblocks
    group_rows = lax.all_gather(amplitudes, "pair", axis=1, tiled=True)[0]
    piece = lax.all_gather(integrals, "grp", axis=0, tiled=True)
    count = piece.shape[0]
    rows = jnp.arange(count, dtype=jnp.int32)
    owner = jnp.take(owner_blocks, rows // sub_width)
    picked = owner * sub_width + rows % sub_width
    chosen = jnp.take(group_rows, picked, axis=1)
    work = jnp.dot(
        chosen, piece, precision=lax.Precision.HIGHEST, preferred_element_type=jnp.float32
    )
    occ_sum = pair_energies(occ_energy, occ_pairs[0])
    vir_local = lax.dynamic_slice_in_dim(vir_pairs, lax.axis_index("pair") * columns, columns, 1)
    vir_sum = pair_energies(vir_energy, vir_local)
    payload = work / (occ_sum[:, None] - vir_sum[None, :])
    return lax.all_to_all(payload[None], "pair", split_axis=1, concat_axis=2, tiled=True)


def solution(mesh):
    body = two_groups if mesh.shape["grp"] == 2 and mesh.shape["pair"] == 16 else any_groups
    return jax.shard_map(
        body,
        mesh=mesh,
        in_specs=(
            P("grp", "pair", None),
            P("grp", "pair"),
            P(),
            P("grp", None, None),
            P(),
            P(),
            P(),
        ),
        out_specs=P("grp", "pair", None),
        check_vma=False,
    )
```
